128 devices in a mesh: lon: 16 (over y, z_hi, core), lat: 8 (over x, z_lo).
Axes of the slice: x: 4, y: 4, z: 4 (z_hi: 2, z_lo: 2; z = z_hi * 2 + z_lo), core: 2. Of those that a mesh axis runs over, the one named last changes fastest.
Arguments:
- adjoint_state: float32 [3, 72, 256, 2048], P(None, None, 'lat', 'lon'), may hold values from -6 to 6
- outflow: float32 [4, 72, 256, 2048], P(None, None, 'lat', 'lon'), may hold values from 0 to 0.25
- mix_blocks: float32 [256, 3, 24, 24], P('lat'), may hold values from -1 to 1
- sounding_owner: int32 [524288, 1], P(('lon', 'lat')), may hold values from 0 to 127; in each aligned block of 4096 rows (0 to 4095, 4096 to 8191, ...) at most 64 rows name the same one
- path_column: int32 [524288, 4], P(('lon', 'lat')), may hold values from 0 to 4095
- path_level: int32 [524288, 3], P(('lon', 'lat')), may hold values from 0 to 72
- kernel_weights: float32 [72, 1048576], P(None, ('lon', 'lat')), may hold values from -0.75 to 0.75
Outputs:
- adjoint_final: float32 [3, 72, 256, 2048], P(None, None, 'lat', 'lon')
- slant_sensitivity: float32 [1048576], P(('lon', 'lat'))
The draws below stay inside these ranges and needn't reach their ends.
Inputs may be any that keep to these rules, and one draw needn't show every extreme that they name: `sounding_owner`: the 4096 soundings of one block name one owner at most 64 times, a bound that some block reaches.
All inputs are finite; a program needn't handle non-finite values.
Results may differ from the reference program's by a relative error of at most 0.0003.
Values sent between devices are 32-bit elements; how exact they have to be, the bound alone decides.
No kernel may reach another device: no remote copies, remote signals or barrier semaphores. Data moves between devices by JAX's collectives and lax.ppermute only.
A program may use at most 192 MiB of HBM per device.

```python
import math
import jax
import jax.numpy as jnp
import numpy as np
from jax import lax

TRACERS = 3
LEVELS = 72
BLOCK = 24
NBLOCKS = 3
CLAT = 32
CLON = 128
STEPS = 2
PATH = 4
SND_SRC = 4096
LAT_BLOCKS = 8
BLOCKS = 128
CAP = 64
OWNER_SLOTS = 8192
NLAT = 256
NLON = 2048
SOUNDINGS = 524288
SLOTS = 1048576


def draw_mix_blocks(key, part):
    key = jax.random.fold_in(key, 11)
    main_key, side_key = jax.random.split(key)
    diagonal = jax.random.uniform(main_key, (NLAT, NBLOCKS, BLOCK), jnp.float32, 0.6, 1.0)
    coupling = jax.random.uniform(side_key, (NLAT, NBLOCKS, BLOCK, BLOCK), jnp.float32, -1.0, 1.0)
    coupling = coupling * (0.4 / math.sqrt(BLOCK))
    identity = jnp.eye(BLOCK, dtype=jnp.float32)
    return coupling * (1.0 - identity) + diagonal[..., :, None] * identity


def place_ends(drawn, rng, least, top_value):
    longest = drawn.shape.index(max(drawn.shape))
    spots = []
    for shift in (0, 1):
        where = [jax.random.randint(jax.random.fold_in(rng, axis), (), 0, length) for axis, length in enumerate(drawn.shape)]
        where[longest] = (where[longest] + shift) % drawn.shape[longest]
        spots.append(tuple(where))
    return drawn.at[spots[0]].set(least).at[spots[1]].set(top_value)


def steps_of(stream_key, extent, cuts, least, high):
    level = 1.0
    for axis_at, parts in cuts:
        heights = jax.random.uniform(jax.random.fold_in(jax.random.fold_in(stream_key, 6), axis_at), (parts,), jnp.float32, least / len(cuts), high / len(cuts))
        level = level * jnp.repeat(jnp.exp(heights), extent[axis_at] // parts).reshape((-1,) + (1,) * (len(extent) - 1 - axis_at))
    return level


def shared_out(key, own, number, rows, number_of, top, limit, skew):
    order = jax.random.permutation(key, number_of)
    crowded, ordinary = shares(number_of, rows * top, limit, skew, True), shares(number_of, rows * top, limit, skew, False)
    places = jnp.arange(number_of)

    def named(lengths, offset_by):
        used = int((lengths > 0).sum())
        fixed = max(1, used // 4)
        passed = fixed + (places - fixed + offset_by * (used - fixed)) % max(1, number_of - fixed)
        return jnp.zeros((number_of,), jnp.int32).at[order[jnp.where(places < fixed, places, passed)]].set(jnp.asarray(lengths, jnp.int32))

    lengths = jnp.where(number % 4 == 0, named(crowded, number // 4), named(ordinary, number - number // 4 - 1))
    mixed = jax.random.permutation(jax.random.fold_in(own, 3), number_of)
    donor, sink = mixed[0:number_of // 2 * 2:2], mixed[1:number_of // 2 * 2:2]
    slack = jnp.minimum(lengths[donor] - 1, limit - lengths[sink]) // 2
    slack = jnp.where((donor == order[0]) | (sink == order[0]) | (lengths[sink] == 0), 0, jnp.maximum(slack, 0))
    passed = jax.random.randint(jax.random.fold_in(own, 4), (number_of // 2,), 0, 1 << 20) % (slack + 1)
    lengths = lengths.at[donor].add(-passed).at[sink].add(passed)
    items = jnp.searchsorted(jnp.cumsum(lengths), jnp.arange(rows * top), side="right").astype(jnp.int32)
    listing = items.reshape(top, rows).T
    listing = listing[jax.random.permutation(jax.random.fold_in(own, 1), rows)]
    offset_by = jax.random.randint(jax.random.fold_in(own, 2), (rows, 1), 0, top)
    return jnp.take_along_axis(listing, (jnp.arange(top)[None, :] + offset_by) % top, axis=1)


def shares(number_of, total, reach, lean, full):
    portions = [(1 << 20) // math.isqrt(grade ** lean) + 1 for grade in range(1, number_of + 1)]
    largest = reach if full else min(reach, max(-(-total // number_of), total * portions[0] // sum(portions)))
    least = 1 if total - largest >= number_of - 1 else 0
    given, spare = [largest] + [least] * (number_of - 1), total - largest - least * (number_of - 1)
    while spare > 0:
        candidates = [i for i in range(1, number_of) if given[i] < largest] or [i for i in range(1, number_of) if given[i] < reach]
        mass, budget = sum([portions[i] for i in candidates]), spare
        for i in candidates:
            extra = min(reach - given[i], max(1, budget * portions[i] // mass), spare)
            given[i] = given[i] + extra
            spare = spare - extra
    return np.array(given)


def noise(own_key, extent, width, bound, cuts=(), held_as=jnp.bfloat16):
    entries = jax.random.normal(own_key, extent, jnp.float32) * width
    if len(cuts) > 0:
        entries = steps_of(own_key, extent, cuts, -0.22, 0.18) * entries
    return jnp.clip(entries, min=-bound, max=bound).astype(held_as)


def setup_inputs(seed: int = 0) -> dict:
    streams_of = jax.random.split(jax.random.key(seed), 8)
    adjoint_state = noise(streams_of[0], (TRACERS, LEVELS, NLAT, NLON), 1.0, 6.0, ((2, 8), (3, 16)), jnp.float32)
    outflow = jnp.clip(0.25 * jax.random.uniform(streams_of[1], (4, LEVELS, NLAT, NLON), jnp.float32) ** steps_of(streams_of[1], (4, LEVELS, NLAT, NLON), ((2, 8), (3, 16)), -0.2, 0.2), 0.0, 0.25)
    mix_blocks = draw_mix_blocks(jax.random.fold_in(streams_of[7], 71), 0)
    sounding_owner_keys = jax.random.split(jax.random.fold_in(streams_of[3], 1), SOUNDINGS // SND_SRC)
    sounding_owner_turns = jax.random.permutation(jax.random.fold_in(streams_of[3], 3), SOUNDINGS // SND_SRC)
    sounding_owner = jax.vmap(lambda own, number: shared_out(jax.random.fold_in(streams_of[3], 2), own, number, SND_SRC, BLOCKS, 1, CAP, 2))(sounding_owner_keys, sounding_owner_turns).reshape((SOUNDINGS, 1))
    path_column = place_ends(jax.random.randint(streams_of[4], (SOUNDINGS, PATH), 0, CLAT * CLON), jax.random.fold_in(streams_of[4], 1), 0, (CLAT * CLON) - 1).astype(jnp.int32)
    path_level = place_ends(jax.random.randint(streams_of[5], (SOUNDINGS, PATH - 1), 0, LEVELS + 1), jax.random.fold_in(streams_of[5], 1), 0, LEVELS).astype(jnp.int32)
    kernel_weights = noise(streams_of[6], (LEVELS, SLOTS), LEVELS ** -0.5, 0.75, ((1, 128),), jnp.float32)
    return {"adjoint_state": adjoint_state, "outflow": outflow, "mix_blocks": mix_blocks, "sounding_owner": sounding_owner, "path_column": path_column, "path_level": path_level, "kernel_weights": kernel_weights}


def advect(tracer, outflow):
    to_east = jnp.roll(tracer, -1, axis=2)
    to_west = jnp.roll(tracer, 1, axis=2)
    zero_row = jnp.zeros_like(tracer[:, :1, :])
    to_north = jnp.concatenate([tracer[:, 1:, :], zero_row], axis=1)
    to_south = jnp.concatenate([zero_row, tracer[:, :-1, :]], axis=1)
    return (tracer + outflow[0] * (to_east - tracer) + outflow[1] * (to_west - tracer)
            + outflow[2] * (to_north - tracer) + outflow[3] * (to_south - tracer))


def mixing(tracer, mix_blocks):
    shaped = tracer.reshape(NBLOCKS, BLOCK, NLAT, NLON)
    mixed_out = jnp.einsum('ybij,biyx->bjyx', mix_blocks, shaped, precision=lax.Precision.HIGHEST)
    return mixed_out.reshape(LEVELS, NLAT, NLON)


def reference(adjoint_state, outflow, mix_blocks, sounding_owner, path_column, path_level, kernel_weights):
    def one_step(tracer):
        return mixing(advect(tracer, outflow), mix_blocks)

    current = adjoint_state
    sampled = adjoint_state
    for step_index in range(STEPS):
        current = lax.map(one_step, current)
        if step_index == 0:
            sampled = current
    column_sum = jnp.sum(sampled, axis=0)
    flat_sum = column_sum.reshape(LEVELS, NLAT * NLON)
    device_id = (jnp.arange(SOUNDINGS, dtype=jnp.int32) // SND_SRC).astype(jnp.int32)
    lat_index = (device_id % LAT_BLOCKS)[:, None] * CLAT + path_column // CLON
    lon_index = (device_id // LAT_BLOCKS)[:, None] * CLON + path_column % CLON
    flat_index = (lat_index * NLON + lon_index).astype(jnp.int32)
    level_ids = jnp.arange(LEVELS, dtype=jnp.int32)
    element = jnp.zeros((LEVELS, SOUNDINGS), jnp.int32)
    for bound_index in range(PATH - 1):
        element = element + (path_level[:, bound_index][None, :] <= level_ids[:, None]).astype(jnp.int32)
    profile = jnp.zeros((LEVELS, SOUNDINGS), flat_sum.dtype)
    for element_index in range(PATH):
        picked = jnp.take(flat_sum, flat_index[:, element_index], axis=1)
        profile = profile + jnp.where(element == element_index, picked, jnp.zeros_like(picked))
    owners = sounding_owner[:, 0].astype(jnp.int32)

    def ranks_of(owner_row):
        onehot = (owner_row[:, None] == jnp.arange(BLOCKS, dtype=jnp.int32)[None, :]).astype(jnp.int32)
        counts = jnp.cumsum(onehot, axis=0).astype(jnp.int32)
        return (jnp.sum(counts * onehot, axis=1) - 1).astype(jnp.int32)

    ranking = lax.map(ranks_of, owners.reshape(BLOCKS, SND_SRC)).reshape(SOUNDINGS).astype(jnp.int32)
    slot_ids = (owners * OWNER_SLOTS + device_id * CAP + ranking).astype(jnp.int32)
    values = jnp.sum(jnp.take(kernel_weights, slot_ids, axis=1) * profile, axis=0)
    sensitivity = jnp.zeros((SLOTS,), values.dtype).at[slot_ids].set(values)
    return current, sensitivity
```

```python
import jax
import jax.numpy as jnp
from jax import lax
from jax.experimental import pallas as pl
from jax.experimental.pallas import tpu as pltpu
from jax.sharding import PartitionSpec as P

T, L, NB, BL, Y, X = 3, 72, 3, 24, 32, 128
OWN, CAP, SND = 128, 64, 4096
YT = Y // 8
K = 8 * BL
ROWS = 40
GROUPS = SND // 128
ATTR = 11
F32, BF16, I32 = jnp.float32, jnp.bfloat16, jnp.int32
VMEM = 56 * 1024 * 1024


def params(*semantics):
    return pltpu.CompilerParams(vmem_limit_bytes=VMEM)


def shape(dims, dtype=F32):
    return jax.ShapeDtypeStruct(dims, dtype)


def iota(dims, dim):
    return lax.broadcasted_iota(I32, dims, dim)


def edges_kernel(v_ref, low_row, high_row, low_col, high_col):
    low_row[...] = v_ref[pl.ds(0, L, stride=Y), :]
    high_row[...] = v_ref[pl.ds(Y - 1, L, stride=Y), :]
    lane = iota((Y, X), 1)
    low = jnp.zeros((Y, X), F32)
    high = jnp.zeros((Y, X), F32)
    for l in range(L):
        turned = pltpu.roll(v_ref[pl.ds(l * Y, Y), :], l, 1)
        low = jnp.where(lane == l, turned, low)
        high = jnp.where(lane == (l + X - 1) % X, turned, high)
    low_col[...] = low
    high_col[...] = pltpu.roll(high, 1, 1)


def edges(state):
    return pl.pallas_call(
        edges_kernel,
        grid=(T,),
        in_specs=[pl.BlockSpec((L * Y, X), lambda t: (t, 0))],
        out_specs=[
            pl.BlockSpec((None, L, X), lambda t: (t, 0, 0)),
            pl.BlockSpec((None, L, X), lambda t: (t, 0, 0)),
            pl.BlockSpec((None, Y, X), lambda t: (t, 0, 0)),
            pl.BlockSpec((None, Y, X), lambda t: (t, 0, 0)),
        ],
        out_shape=[shape((T, L, X)), shape((T, L, X)), shape((T, Y, X)), shape((T, Y, X))],
        compiler_params=params(),
        name="edges",
    )(state.reshape(T * L * Y, X))


def exchange(low_row, high_row, low_col, high_col):
    lats, lons = lax.axis_size("lat"), lax.axis_size("lon")
    up = [(i, i + 1) for i in range(lats - 1)]
    down = [(b, a) for a, b in up]
    east = [(i, (i + 1) % lons) for i in range(lons)]
    west = [(b, a) for a, b in east]
    north = lax.ppermute(low_row, "lat", down)
    south = lax.ppermute(high_row, "lat", up)
    to_east = lax.ppermute(low_col, "lon", west)
    to_west = lax.ppermute(high_col, "lon", east)
    return north, south, to_east, to_west


def spread_kernel(r_ref, hi_ref, lo_ref):
    same = iota((K, K), 0) % 8 == iota((K, K), 1) % 8
    pick = jnp.where(iota((BL, K), 0) == iota((BL, K), 1) // 8, 1.0, 0.0).astype(BF16)
    for n in range(NB * YT):
        r = jnp.concatenate([r_ref[n, pl.ds(j, 8, stride=BL), :] for j in range(BL)], axis=0)
        for part, ref in zip(split(r), (hi_ref, lo_ref)):
            wide = jnp.dot(part, pick, preferred_element_type=F32)
            ref[n] = jnp.where(same, wide, 0.0).astype(BF16)


def spread(r):
    return pl.pallas_call(
        spread_kernel,
        out_shape=[shape((NB * YT, K, K), BF16)] * 2,
        compiler_params=params(),
        name="spread",
    )(r)


def transported(v, flows, north, south, to_east, to_west):
    row, lane = iota((Y, X), 0), iota((Y, X), 1)
    e = jnp.where(lane == X - 1, to_east, pltpu.roll(v, X - 1, 1))
    w = jnp.where(lane == 0, to_west, pltpu.roll(v, 1, 1))
    n = jnp.where(row == Y - 1, north, pltpu.roll(v, Y - 1, 0))
    s = jnp.where(row == 0, south, pltpu.roll(v, 1, 0))
    return v + flows[0] * (e - v) + flows[1] * (w - v) + flows[2] * (n - v) + flows[3] * (s - v)


def split(x):
    hi = x.astype(BF16)
    return hi, (x - hi.astype(F32)).astype(BF16)


def mixed(hi, lo, x):
    x_hi, x_lo = split(x)
    dot = lambda a, b: jnp.dot(a, b, preferred_element_type=F32)
    return dot(hi, x_hi) + (dot(hi, x_lo) + dot(lo, x_hi))


def step_specs():
    return [
        pl.BlockSpec((T, BL, Y, X), lambda b: (0, b, 0, 0)),
        pl.BlockSpec((4, BL, Y, X), lambda b: (0, b, 0, 0)),
        pl.BlockSpec((T, BL, X), lambda b: (0, b, 0)),
        pl.BlockSpec((T, BL, X), lambda b: (0, b, 0)),
        pl.BlockSpec((T, Y, X), lambda b: (0, 0, 0)),
        pl.BlockSpec((T, Y, X), lambda b: (0, 0, 0)),
        pl.BlockSpec((YT, K, K), lambda b: (b, 0, 0)),
        pl.BlockSpec((YT, K, K), lambda b: (b, 0, 0)),
    ]


def step_kernel(extras, v_ref, f_ref, n_ref, s_ref, e_ref, w_ref, hi_ref, lo_ref, out_ref, *rest):
    b = pl.program_id(0)
    adv = rest[-1]
    for t in range(T):
        for i in range(BL):
            l = b * BL + i
            a = transported(
                v_ref[t, i],
                [f_ref[k, i] for k in range(4)],
                n_ref[t, pl.ds(i, 1), :],
                s_ref[t, pl.ds(i, 1), :],
                pltpu.roll(e_ref[t], X - 1 - l, 1),
                pltpu.roll(w_ref[t], X - l, 1),
            )
            for q in range(YT):
                adv[q, pl.ds(i * 8, 8), pl.ds(t * X, X)] = a[q * 8 : q * 8 + 8]
    if extras:
        table, low_row, high_row, low_col, high_col, summed, _ = rest
        lane = iota((8, X), 1)

        @pl.when(b == 0)
        def _():
            low_col[...] = jnp.zeros((T, Y, X), F32)
            high_col[...] = jnp.zeros((T, Y, X), F32)

    for q in range(YT):
        out = mixed(hi_ref[q], lo_ref[q], adv[q])
        parts = [
            [out[j * 8 : j * 8 + 8, t * X : (t + 1) * X] for j in range(BL)] for t in range(T)
        ]
        for t in range(T):
            for j in range(BL):
                out_ref[t, j, pl.ds(q * 8, 8), :] = parts[t][j]
        if extras:
            here = pl.ds(q * 8, 8)
            for j in range(BL):
                summed[pl.ds(j * Y + q * 8, 8), :] = parts[0][j] + parts[1][j] + parts[2][j]
            for t in range(T):
                low, high = low_col[t, here, :], high_col[t, here, :]
                for j in range(BL):
                    l = b * BL + j
                    low = jnp.where(lane == l, pltpu.roll(parts[t][j], l, 1), low)
                    high = jnp.where(lane == l, pltpu.roll(parts[t][j], l + 1, 1), high)
                low_col[t, here, :] = low
                high_col[t, here, :] = high
    if extras:
        for y in range(Y):
            table[y] = summed[pl.ds(y, BL, stride=Y), :]
        for t in range(T):
            low_row[t] = out_ref[t, :, 0, :]
            high_row[t] = out_ref[t, :, Y - 1, :]


def full_step(state, outflow, halo, matrices, extras):
    def kernel(*refs):
        step_kernel(extras, *refs)

    out_specs = [pl.BlockSpec((T, BL, Y, X), lambda b: (0, b, 0, 0))]
    out_shape = [shape((T, L, Y, X))]
    scratch = [pltpu.VMEM((YT, K, T * X), F32)]
    if extras:
        out_specs += [
            pl.BlockSpec((Y, BL, X), lambda b: (0, b, 0)),
            pl.BlockSpec((T, BL, X), lambda b: (0, b, 0)),
            pl.BlockSpec((T, BL, X), lambda b: (0, b, 0)),
            pl.BlockSpec((T, Y, X), lambda b: (0, 0, 0)),
            pl.BlockSpec((T, Y, X), lambda b: (0, 0, 0)),
        ]
        out_shape += [
            shape((Y, L, X)),
            shape((T, L, X)),
            shape((T, L, X)),
            shape((T, Y, X)),
            shape((T, Y, X)),
        ]
        scratch = [pltpu.VMEM((BL * Y, X), F32)] + scratch
    return pl.pallas_call(
        kernel,
        grid=(NB,),
        in_specs=step_specs(),
        out_specs=out_specs,
        out_shape=out_shape,
        scratch_shapes=scratch,
        compiler_params=params(),
        name="step",
    )(state, outflow, *halo, *matrices)


def order_kernel(own_ref, col_ref, lev_ref, pc_ref, pv_ref, start_ref, count_ref, place):
    width = 256
    chunks = SND // width
    owner = iota((OWN, width), 0)
    named = lambda c: owner == own_ref[:, pl.ds(c * width, width)]
    bit = lambda m: jnp.where(m, 1.0, 0.0).astype(BF16)
    upto = bit(iota((width, width), 0) <= iota((width, width), 1))
    ones = jnp.ones((width, width), BF16)
    ones_rows = jnp.ones((16, width), BF16)
    total = jnp.zeros((OWN, width), F32)
    total_row = jnp.zeros((16, OWN), F32)
    over_lanes = (((1,), (1,)), ((), ()))
    for c in range(chunks):
        hot = bit(named(c))
        total = total + jnp.dot(hot, ones, preferred_element_type=F32)
        total_row = total_row + lax.dot_general(
            ones_rows, hot, over_lanes, preferred_element_type=F32
        )
    below = bit(iota((OWN, OWN), 1) < iota((OWN, OWN), 0))
    before = bit(iota((OWN, OWN), 0) < iota((OWN, OWN), 1))
    base = jnp.dot(below, total.astype(BF16), preferred_element_type=F32)
    start_row = jnp.dot(total_row.astype(BF16), before, preferred_element_type=F32)
    start_ref[...] = start_row[0:1].astype(I32)
    count_ref[...] = total_row[0:1].astype(I32)
    for c in range(chunks):
        m = named(c)
        hot = bit(m)
        upto_here = jnp.dot(hot, upto, preferred_element_type=F32) + base
        spot = jnp.sum(jnp.where(m, upto_here, 0.0), axis=0, keepdims=True) - 1.0
        place[:, pl.ds(c * width, width)] = spot.astype(I32)
        base = base + jnp.dot(hot, ones, preferred_element_type=F32)
    width = 512
    sorted_ = jnp.zeros((ATTR * GROUPS, 128), F32)
    for c in range(SND // width):
        here = pl.ds(c * width, width)
        spot = place[:, here]
        group = iota((GROUPS, width), 0) == spot // 128
        lane = bit(iota((128, width), 0) == spot % 128)
        rows = []
        for a in range(4):
            rows.append(col_ref[a : a + 1, here] // 128)
        for a in range(4):
            rows.append(col_ref[a : a + 1, here] % 128)
        for a in range(3):
            rows.append(lev_ref[a : a + 1, here])
        spread_rows = jnp.concatenate(
            [jnp.where(group, r.astype(F32), 0.0) for r in rows], axis=0
        ).astype(BF16)
        sorted_ = sorted_ + lax.dot_general(
            spread_rows, lane, over_lanes, preferred_element_type=F32
        )
    for a in range(4):
        y = sorted_[a * GROUPS : (a + 1) * GROUPS]
        x = sorted_[(a + 4) * GROUPS : (a + 5) * GROUPS]
        pc_ref[a] = (y * 128.0 + x).astype(I32)
        pc_ref[a + 4] = pltpu.roll(pc_ref[a], 64, 1)
    for a in range(3):
        pv_ref[a] = sorted_[(a + 8) * GROUPS : (a + 9) * GROUPS].astype(I32)
        pv_ref[a + 3] = pltpu.roll(pv_ref[a], 64, 1)


def order(owner, path_column, path_level):
    return pl.pallas_call(
        order_kernel,
        out_shape=[
            shape((8, GROUPS, 128), I32),
            shape((6, GROUPS, 128), I32),
            shape((1, OWN), I32),
            shape((1, OWN), I32),
        ],
        scratch_shapes=[pltpu.VMEM((1, SND), I32)],
        compiler_params=params(),
        name="order",
    )(owner.reshape(1, SND), path_column.T, path_level.T)


def sample_kernel(table, pc_ref, pv_ref, found):
    def sample(g, carry):
        for k in range(L // 8):
            swap = 0 if k < 5 else 1
            cols = [pc_ref[a + 4 * swap, pl.ds(g, 1), :] for a in range(4)]
            levs = [pv_ref[a + 3 * swap, pl.ds(g, 1), :] for a in range(3)]
            level = iota((8, 128), 0) + k * 8
            passed = [jnp.where(v <= level, 1, 0) for v in levs]
            element = passed[0] + passed[1] + passed[2]
            at = jnp.where(
                element < 2,
                jnp.where(element < 1, cols[0], cols[1]),
                jnp.where(element < 3, cols[2], cols[3]),
            )
            x, y = at & 127, at >> 7
            acc = jnp.zeros((8, 128), F32)
            for row in range(Y):
                got = jnp.take_along_axis(
                    table[row, k * 8 : k * 8 + 8, :], x, axis=1, mode="promise_in_bounds"
                )
                acc = jnp.where(y == row, got, acc)
            found[g, k * 8 : k * 8 + 8, :] = acc
        return carry

    lax.fori_loop(0, GROUPS, sample, 0)
    found[GROUPS] = jnp.zeros((L, 128), F32)


def sampled(table, pc, pv):
    return pl.pallas_call(
        sample_kernel,
        out_shape=shape((GROUPS + 1, L, 128)),
        compiler_params=params(),
        name="sample",
    )(table, pc, pv)


def pack_kernel(k_ref, out_ref):
    first = iota((8, 128), 1) < 64
    for pair in range(16):
        lanes = slice(pair * 128, (pair + 1) * 128)
        for k in range(5):
            low = k_ref[k * 8 : k * 8 + 8, lanes]
            if k < 4:
                high = pltpu.roll(k_ref[(k + 5) * 8 : (k + 6) * 8, lanes], 64, 1)
            else:
                high = jnp.zeros((8, 128), F32)
            out_ref[2 * pair, k * 8 : k * 8 + 8, :] = jnp.where(first, low, high)
            out_ref[2 * pair + 1, k * 8 : k * 8 + 8, :] = jnp.where(first, high, low)


def packed_weights(weights):
    return pl.pallas_call(
        pack_kernel,
        grid=(OWN // 32,),
        in_specs=[pl.BlockSpec((L, 2048), lambda i: (0, i))],
        out_specs=pl.BlockSpec((32, ROWS, 128), lambda i: (i, 0, 0)),
        out_shape=shape((OWN, ROWS, 128)),
        compiler_params=params(),
        name="pack",
    )(weights)


def weigh_kernel(start_ref, count_ref, half_ref, found, k_ref, out_ref, kept):
    lane = iota((8, 128), 1)
    step = pl.program_id(0)
    for n in range(16):
        o = step * 16 + n
        start, count = start_ref[0, o], count_ref[0, o]
        group, offset = jnp.minimum(start // 128, GROUPS - 1), start % 128
        near = lane >= offset
        near_high = (lane ^ 64) >= offset
        low = ((lane - offset) & 127) < 64
        acc = jnp.zeros((8, 128), F32)
        for k in range(5):
            rows = slice(k * 8, k * 8 + 8)
            z = jnp.where(near, found[group, rows, :], found[group + 1, rows, :])
            if k < 4:
                rows_high = slice((k + 5) * 8, (k + 6) * 8)
                z_high = jnp.where(
                    near_high, found[group, rows_high, :], found[group + 1, rows_high, :]
                )
                z = jnp.where(low, z, z_high)
            turned = pltpu.roll(z, (half_ref[0] + 128 - offset) % 128, 1)
            acc = acc + turned * k_ref[n, rows, :]
        kept[pl.ds(n * 8, 8), :] = jnp.where((lane & 63) < count, acc, 0.0)
    total = kept[pl.ds(0, 16, stride=8), :]
    for r in range(1, 8):
        total = total + kept[pl.ds(r, 16, stride=8), :]
    out_ref[...] = total + pltpu.roll(total, 64, 1)


def weigh(start, count, half, found, arrived):
    smem = pl.BlockSpec(memory_space=pltpu.SMEM)
    return pl.pallas_call(
        weigh_kernel,
        grid=(OWN // 16,),
        in_specs=[
            smem,
            smem,
            smem,
            pl.BlockSpec((GROUPS + 1, L, 128), lambda i: (0, 0, 0)),
            pl.BlockSpec((16, ROWS, 128), lambda i: (i, 0, 0)),
        ],
        out_specs=pl.BlockSpec((16, 128), lambda i: (i, 0)),
        out_shape=shape((OWN, 128)),
        scratch_shapes=[pltpu.VMEM((128, 128), F32)],
        compiler_params=params(),
        name="weigh",
    )(start, count, half, found, arrived)


def body(state, outflow, mix_blocks, owner, path_column, path_level, weights):
    axes = ("lon", "lat")
    sides = edges(state)
    halo = exchange(*sides)
    packed, halo = lax.optimization_barrier((packed_weights(weights), halo))
    arrived = lax.all_to_all(packed, axes, 0, 0, tiled=True)
    rows = mix_blocks.reshape(YT, 8, NB, BL, BL).transpose(2, 0, 1, 4, 3)
    matrices = spread(rows.reshape(NB * YT, K, BL))
    pc, pv, start, count = order(owner, path_column, path_level)
    half = (lax.axis_index("lat") % 2 * 64).astype(I32).reshape(1)
    first, table, *sides = full_step(state, outflow, halo, matrices, True)
    found = sampled(table, pc, pv)
    sums = weigh(start, count, half, found, arrived)
    sensitivity = lax.all_to_all(sums, axes, 0, 0, tiled=True)[:, :CAP]
    (final,) = full_step(first, outflow, exchange(*sides), matrices, False)
    return final, sensitivity.reshape(OWN * CAP)


def solution(mesh):
    return jax.shard_map(
        body,
        mesh=mesh,
        in_specs=(
            P(None, None, "lat", "lon"),
            P(None, None, "lat", "lon"),
            P("lat", None, None, None),
            P(("lon", "lat"), None),
            P(("lon", "lat"), None),
            P(("lon", "lat"), None),
            P(None, ("lon", "lat")),
        ),
        out_specs=(P(None, None, "lat", "lon"), P(("lon", "lat"))),
        check_vma=False,
    )
```

```python
import jax
import jax.numpy as jnp
from jax import lax
from jax.experimental import pallas as pl
from jax.experimental.pallas import tpu as pltpu
from jax.sharding import PartitionSpec as P

T, L, NB, BL, Y, X = 3, 72, 3, 24, 32, 128
OWN, CAP, SND = 128, 64, 4096
YT = Y // 8
K = 8 * BL
ROWS = 40
GROUPS = SND // 128
ATTR = 11
F32, BF16, I32 = jnp.float32, jnp.bfloat16, jnp.int32
VMEM = 63 * 1024 * 1024


def params(*semantics):
    return pltpu.CompilerParams(vmem_limit_bytes=VMEM)


def shape(dims, dtype=F32):
    return jax.ShapeDtypeStruct(dims, dtype)


def iota(dims, dim):
    return lax.broadcasted_iota(I32, dims, dim)


def copies(pairs, sems):
    return [pltpu.make_async_copy(src, dst, sems.at[n]) for n, (src, dst) in enumerate(pairs)]


ANY = pl.BlockSpec(memory_space=pl.ANY)
IN_VMEM = pl.BlockSpec(memory_space=pltpu.VMEM)
IN_SMEM = pl.BlockSpec(memory_space=pltpu.SMEM)


def edge_columns(parts):
    lane = iota((parts[0].shape[0], X), 1)
    both = jnp.zeros(lane.shape, F32)
    for i, part in enumerate(parts):
        both = jnp.where(lane >> 1 == i, pltpu.roll(part, 2 * i + 1, 1), both)
    return both


PACKS = 4


def prepare_kernel(v_hbm, k_hbm, low_row, high_row, cols, packed_hbm, v, k, packed, v_sem, k_sem, p_sem):
    wide = OWN * CAP // PACKS
    deep = OWN // PACKS
    v_in = copies([(v_hbm.at[t], v.at[t]) for t in range(T)], v_sem)
    k_in = copies([(k_hbm.at[:, pl.ds(n * wide, wide)], k.at[n]) for n in range(PACKS)], k_sem)
    out = copies(
        [(packed.at[n], packed_hbm.at[pl.ds(n * deep, deep)]) for n in range(PACKS)], p_sem
    )
    for c in v_in + k_in:
        c.start()
    for t in range(T):
        v_in[t].wait()
        low_row[t] = v[t, pl.ds(0, L, stride=Y), :]
        high_row[t] = v[t, pl.ds(Y - 1, L, stride=Y), :]
        for b in range(NB):
            cols[b, t] = edge_columns([v[t, pl.ds((b * BL + i) * Y, Y), :] for i in range(BL)])
    first = iota((8, 128), 1) < 64
    for n in range(PACKS):
        k_in[n].wait()
        for pair in range(deep // 2):
            lanes = slice(pair * 128, (pair + 1) * 128)
            for r in range(5):
                low = k[n, r * 8 : r * 8 + 8, lanes]
                if r < 4:
                    high = pltpu.roll(k[n, (r + 5) * 8 : (r + 6) * 8, lanes], 64, 1)
                else:
                    high = jnp.zeros((8, 128), F32)
                packed[n, 2 * pair, r * 8 : r * 8 + 8, :] = jnp.where(first, low, high)
                packed[n, 2 * pair + 1, r * 8 : r * 8 + 8, :] = jnp.where(first, high, low)
        out[n].start()
    for c in out:
        c.wait()


def prepare(state, weights):
    return pl.pallas_call(
        prepare_kernel,
        in_specs=[ANY, ANY],
        out_specs=[IN_VMEM, IN_VMEM, IN_VMEM, ANY],
        out_shape=[
            shape((T, L, X)),
            shape((T, L, X)),
            shape((NB, T, Y, X)),
            shape((OWN, ROWS, 128)),
        ],
        scratch_shapes=[
            pltpu.VMEM((T, L * Y, X), F32),
            pltpu.VMEM((PACKS, L, OWN * CAP // PACKS), F32),
            pltpu.VMEM((PACKS, OWN // PACKS, ROWS, 128), F32),
            pltpu.SemaphoreType.DMA((T,)),
            pltpu.SemaphoreType.DMA((PACKS,)),
            pltpu.SemaphoreType.DMA((PACKS,)),
        ],
        compiler_params=params(),
        name="prepare",
    )(state.reshape(T, L * Y, X), weights)


def exchange(low_row, high_row, cols):
    lats, lons = lax.axis_size("lat"), lax.axis_size("lon")
    up = [(i, i + 1) for i in range(lats - 1)]
    down = [(b, a) for a, b in up]
    east = [(i, (i + 1) % lons) for i in range(lons)]
    west = [(b, a) for a, b in east]
    north = lax.ppermute(low_row, "lat", down)
    south = lax.ppermute(high_row, "lat", up)
    from_east = lax.ppermute(cols, "lon", west)
    from_west = lax.ppermute(cols, "lon", east)
    return north, south, from_east, from_west


def split(x):
    hi = x.astype(BF16)
    return hi, (x - hi.astype(F32)).astype(BF16)


def spread(r_ref, hi_ref, lo_ref):
    same = iota((K, K), 0) % 8 == iota((K, K), 1) % 8
    pick = jnp.where(iota((BL, K), 0) == iota((BL, K), 1) // 8, 1.0, 0.0).astype(BF16)
    for n in range(NB * YT):
        r = jnp.concatenate([r_ref[n, pl.ds(j, 8, stride=BL), :] for j in range(BL)], axis=0)
        for part, ref in zip(split(r), (hi_ref, lo_ref)):
            wide = jnp.dot(part, pick, preferred_element_type=F32)
            ref[n] = jnp.where(same, wide, 0.0).astype(BF16)


def transported(v, flows, north, south, sides):
    row, lane = iota((Y, X), 0), iota((Y, X), 1)
    e = pltpu.roll(jnp.where(lane == 0, sides, v), X - 1, 1)
    w = pltpu.roll(jnp.where(lane == X - 1, sides, v), 1, 1)
    n = jnp.where(row == Y - 1, north, pltpu.roll(v, Y - 1, 0))
    s = jnp.where(row == 0, south, pltpu.roll(v, 1, 0))
    return v + flows[0] * (e - v) + flows[1] * (w - v) + flows[2] * (n - v) + flows[3] * (s - v)


def mixed(hi, lo, x):
    x_hi, x_lo = split(x)
    dot = lambda a, b: jnp.dot(a, b, preferred_element_type=F32)
    return dot(hi, x_hi) + (dot(hi, x_lo) + dot(lo, x_hi))


def transport_block(adv, v, f, n_ref, s_ref, e_ref, w_ref):
    odd = (iota((Y, X), 1) & 1) == 1
    for t in range(T):
        sides = jnp.where(odd, e_ref[t], w_ref[t])
        for i in range(BL):
            a = transported(
                v[t, i],
                [f[k, i] for k in range(4)],
                n_ref[t, pl.ds(i, 1), :],
                s_ref[t, pl.ds(i, 1), :],
                pltpu.roll(sides, (X - 2 * i - 1) % X, 1),
            )
            for q in range(YT):
                adv[q, pl.ds(i * 8, 8), pl.ds(t * X, X)] = a[q * 8 : q * 8 + 8]


def tiles(out):
    return [[out[j * 8 : j * 8 + 8, t * X : (t + 1) * X] for j in range(BL)] for t in range(T)]


def last_kernel(v_ref, f_ref, n_ref, s_ref, e_ref, w_ref, hi_ref, lo_ref, out_ref, adv):
    transport_block(adv, v_ref, f_ref, n_ref, s_ref, e_ref, w_ref)
    for q in range(YT):
        parts = tiles(mixed(hi_ref[q], lo_ref[q], adv[q]))
        for t in range(T):
            for j in range(BL):
                out_ref[t, j, pl.ds(q * 8, 8), :] = parts[t][j]


def last_step(state, outflow, halo, matrices):
    return pl.pallas_call(
        last_kernel,
        grid=(NB,),
        in_specs=[
            pl.BlockSpec((T, BL, Y, X), lambda b: (0, b, 0, 0)),
            pl.BlockSpec((4, BL, Y, X), lambda b: (0, b, 0, 0)),
            pl.BlockSpec((T, BL, X), lambda b: (0, b, 0)),
            pl.BlockSpec((T, BL, X), lambda b: (0, b, 0)),
            pl.BlockSpec((None, T, Y, X), lambda b: (b, 0, 0, 0)),
            pl.BlockSpec((None, T, Y, X), lambda b: (b, 0, 0, 0)),
            pl.BlockSpec((YT, K, K), lambda b: (b, 0, 0)),
            pl.BlockSpec((YT, K, K), lambda b: (b, 0, 0)),
        ],
        out_specs=pl.BlockSpec((T, BL, Y, X), lambda b: (0, b, 0, 0)),
        out_shape=shape((T, L, Y, X)),
        scratch_shapes=[pltpu.VMEM((YT, K, T * X), F32)],
        compiler_params=params(),
        name="last_step",
    )(state, outflow, *halo, *matrices)


def order(own_ref, col_ref, lev_ref, pc_ref, pv_ref, start_ref, count_ref, place):
    width = 256
    chunks = SND // width
    owner = iota((OWN, width), 0)
    named = lambda c: owner == own_ref[:, pl.ds(c * width, width)]
    bit = lambda m: jnp.where(m, 1.0, 0.0).astype(BF16)
    upto = bit(iota((width, width), 0) <= iota((width, width), 1))
    ones = jnp.ones((width, width), BF16)
    ones_rows = jnp.ones((16, width), BF16)
    total = jnp.zeros((OWN, width), F32)
    total_row = jnp.zeros((16, OWN), F32)
    over_lanes = (((1,), (1,)), ((), ()))
    for c in range(chunks):
        hot = bit(named(c))
        total = total + jnp.dot(hot, ones, preferred_element_type=F32)
        total_row = total_row + lax.dot_general(
            ones_rows, hot, over_lanes, preferred_element_type=F32
        )
    below = bit(iota((OWN, OWN), 1) < iota((OWN, OWN), 0))
    before = bit(iota((OWN, OWN), 0) < iota((OWN, OWN), 1))
    base = jnp.dot(below, total.astype(BF16), preferred_element_type=F32)
    start_row = jnp.dot(total_row.astype(BF16), before, preferred_element_type=F32)
    start_ref[...] = start_row[0:1].astype(I32)
    count_ref[...] = total_row[0:1].astype(I32)
    for c in range(chunks):
        m = named(c)
        hot = bit(m)
        upto_here = jnp.dot(hot, upto, preferred_element_type=F32) + base
        spot = jnp.sum(jnp.where(m, upto_here, 0.0), axis=0, keepdims=True) - 1.0
        place[:, pl.ds(c * width, width)] = spot.astype(I32)
        base = base + jnp.dot(hot, ones, preferred_element_type=F32)
    width = 512
    sorted_ = jnp.zeros((ATTR * GROUPS, 128), F32)
    for c in range(SND // width):
        here = pl.ds(c * width, width)
        spot = place[:, here]
        group = iota((GROUPS, width), 0) == spot // 128
        lane = bit(iota((128, width), 0) == spot % 128)
        rows = []
        for a in range(4):
            rows.append(col_ref[a : a + 1, here] // 128)
        for a in range(4):
            rows.append(col_ref[a : a + 1, here] % 128)
        for a in range(3):
            rows.append(lev_ref[a : a + 1, here])
        spread_rows = jnp.concatenate(
            [jnp.where(group, r.astype(F32), 0.0) for r in rows], axis=0
        ).astype(BF16)
        sorted_ = sorted_ + lax.dot_general(
            spread_rows, lane, over_lanes, preferred_element_type=F32
        )
    for a in range(4):
        y = sorted_[a * GROUPS : (a + 1) * GROUPS]
        x = sorted_[(a + 4) * GROUPS : (a + 5) * GROUPS]
        pc_ref[a] = (y * 128.0 + x).astype(I32)
        pc_ref[a + 4] = pltpu.roll(pc_ref[a], 64, 1)
    for a in range(3):
        pv_ref[a] = sorted_[(a + 8) * GROUPS : (a + 9) * GROUPS].astype(I32)
        pv_ref[a + 3] = pltpu.roll(pv_ref[a], 64, 1)


def sample_all(table, pc_ref, pv_ref, found):
    def sample(g, carry):
        for k in range(L // 8):
            swap = 0 if k < 5 else 1
            cols = [pc_ref[a + 4 * swap, pl.ds(g, 1), :] for a in range(4)]
            levs = [pv_ref[a + 3 * swap, pl.ds(g, 1), :] for a in range(3)]
            level = iota((8, 128), 0) + k * 8
            passed = [jnp.where(v <= level, 1, 0) for v in levs]
            element = passed[0] + passed[1] + passed[2]
            at = jnp.where(
                element < 2,
                jnp.where(element < 1, cols[0], cols[1]),
                jnp.where(element < 3, cols[2], cols[3]),
            )
            x, y = at & 127, at >> 7
            acc = jnp.zeros((8, 128), F32)
            for row in range(Y):
                got = jnp.take_along_axis(
                    table[row, k * 8 : k * 8 + 8, :], x, axis=1, mode="promise_in_bounds"
                )
                acc = jnp.where(y == row, got, acc)
            found[g, k * 8 : k * 8 + 8, :] = acc
        return carry

    lax.fori_loop(0, GROUPS, sample, 0)
    found[GROUPS] = jnp.zeros((L, 128), F32)


def first_kernel(
    v_hbm, f_hbm, r_ref, own_ref, col_ref, lev_ref, n_ref, s_ref, e_ref, w_ref,
    out_hbm, hi_hbm, lo_hbm, low_row, high_row, cols, found, start_ref, count_ref,
    v, f, out, hi, lo, table, adv, summed, pc, pv, place, v_sem, f_sem, o_sem, m_sem,
):
    levels = [pl.ds(b * BL, BL) for b in range(NB)]
    v_in = copies([(v_hbm.at[:, d], v.at[b]) for b, d in enumerate(levels)], v_sem)
    f_in = copies([(f_hbm.at[:, d], f.at[b]) for b, d in enumerate(levels)], f_sem)
    outs = copies([(out.at[b], out_hbm.at[:, d]) for b, d in enumerate(levels)], o_sem)
    made = copies([(hi, hi_hbm), (lo, lo_hbm)], m_sem)
    for b in range(NB):
        v_in[b].start()
        f_in[b].start()
    spread(r_ref, hi, lo)
    for c in made:
        c.start()
    order(own_ref, col_ref, lev_ref, pc, pv, start_ref, count_ref, place)
    for b in range(NB):
        v_in[b].wait()
        f_in[b].wait()
        here = levels[b]
        transport_block(
            adv, v.at[b], f.at[b], n_ref.at[:, here], s_ref.at[:, here], e_ref.at[b], w_ref.at[b]
        )
        for q in range(YT):
            parts = tiles(mixed(hi[b * YT + q], lo[b * YT + q], adv[q]))
            rows = pl.ds(q * 8, 8)
            for t in range(T):
                for j in range(BL):
                    out[b, t, j, rows, :] = parts[t][j]
                cols[b, t, rows, :] = edge_columns(parts[t])
            for j in range(BL):
                summed[pl.ds(j * Y + q * 8, 8), :] = parts[0][j] + parts[1][j] + parts[2][j]
        for y in range(Y):
            table[y, here, :] = summed[pl.ds(y, BL, stride=Y), :]
        for t in range(T):
            low_row[t, here, :] = out[b, t, :, 0, :]
            high_row[t, here, :] = out[b, t, :, Y - 1, :]
        outs[b].start()
    sample_all(table, pc, pv, found)
    for c in outs + made:
        c.wait()


def first_step(state, outflow, rows, owner, path_column, path_level, halo):
    vmem = lambda dims, dtype=F32: pltpu.VMEM(dims, dtype)
    return pl.pallas_call(
        first_kernel,
        in_specs=[ANY, ANY] + [IN_VMEM] * 8,
        out_specs=[ANY, ANY, ANY] + [IN_VMEM] * 6,
        out_shape=[
            shape((T, L, Y, X)),
            shape((NB * YT, K, K), BF16),
            shape((NB * YT, K, K), BF16),
            shape((T, L, X)),
            shape((T, L, X)),
            shape((NB, T, Y, X)),
            shape((GROUPS + 1, L, 128)),
            shape((1, OWN), I32),
            shape((1, OWN), I32),
        ],
        scratch_shapes=[
            vmem((NB, T, BL, Y, X)),
            vmem((NB, 4, BL, Y, X)),
            vmem((NB, T, BL, Y, X)),
            vmem((NB * YT, K, K), BF16),
            vmem((NB * YT, K, K), BF16),
            vmem((Y, L, X)),
            vmem((YT, K, T * X)),
            vmem((BL * Y, X)),
            vmem((8, GROUPS, 128), I32),
            vmem((6, GROUPS, 128), I32),
            vmem((1, SND), I32),
            pltpu.SemaphoreType.DMA((NB,)),
            pltpu.SemaphoreType.DMA((NB,)),
            pltpu.SemaphoreType.DMA((NB,)),
            pltpu.SemaphoreType.DMA((2,)),
        ],
        compiler_params=params(),
        name="first_step",
    )(state, outflow, rows, owner.reshape(1, SND), path_column.T, path_level.T, *halo)


def weigh_kernel(
    start_ref, count_ref, half_ref, found_hbm, k_hbm, out_ref, found, k, kept, found_sem, k_sem
):
    deep = OWN // PACKS
    k_in = copies([(k_hbm.at[pl.ds(c * deep, deep)], k.at[c]) for c in range(PACKS)], k_sem)
    (found_in,) = copies([(found_hbm, found)], found_sem)
    found_in.start()
    for c in k_in:
        c.start()
    found_in.wait()
    lane = iota((8, 128), 1)
    many = 8
    for c in range(PACKS):
        k_in[c].wait()

        def some(step, carry):
            sums = []
            for n in range(many):
                o = c * deep + step * many + n
                start, count = start_ref[0, o], count_ref[0, o]
                group, offset = jnp.minimum(start >> 7, GROUPS - 1), start & 127
                near = lane >= offset
                near_high = (lane ^ 64) >= offset
                low = ((lane - offset) & 127) < 64
                acc = jnp.zeros((8, 128), F32)
                for r in range(5):
                    rows = slice(r * 8, r * 8 + 8)
                    z = jnp.where(near, found[group, rows, :], found[group + 1, rows, :])
                    if r < 4:
                        high = slice((r + 5) * 8, (r + 6) * 8)
                        z_high = jnp.where(
                            near_high, found[group, high, :], found[group + 1, high, :]
                        )
                        z = jnp.where(low, z, z_high)
                    turned = pltpu.roll(z, (half_ref[0] + 128 - offset) & 127, 1)
                    acc = acc + turned * k[c, step * many + n, rows, :]
                sums.append(jnp.where((lane & 63) < count, acc, 0.0))
            for n in range(many):
                kept[pl.ds((c * deep + step * many + n) * 8, 8), :] = sums[n]
            return carry

        lax.fori_loop(0, deep // many, some, 0)
    total = kept[pl.ds(0, OWN, stride=8), :]
    for r in range(1, 8):
        total = total + kept[pl.ds(r, OWN, stride=8), :]
    out_ref[...] = total + pltpu.roll(total, 64, 1)


def weigh(start, count, half, found, arrived):
    return pl.pallas_call(
        weigh_kernel,
        in_specs=[IN_SMEM, IN_SMEM, IN_SMEM, ANY, ANY],
        out_specs=IN_VMEM,
        out_shape=shape((OWN, 128)),
        scratch_shapes=[
            pltpu.VMEM((GROUPS + 1, L, 128), F32),
            pltpu.VMEM((PACKS, OWN // PACKS, ROWS, 128), F32),
            pltpu.VMEM((OWN * 8, 128), F32),
            pltpu.SemaphoreType.DMA((1,)),
            pltpu.SemaphoreType.DMA((PACKS,)),
        ],
        compiler_params=params(),
        name="weigh",
    )(start, count, half, found, arrived)


def body(state, outflow, mix_blocks, owner, path_column, path_level, weights):
    axes = ("lon", "lat")
    *sides, packed = prepare(state, weights)
    packed, halo = lax.optimization_barrier((packed, exchange(*sides)))
    arrived = lax.all_to_all(packed, axes, 0, 0, tiled=True)
    rows = mix_blocks.reshape(YT, 8, NB, BL, BL).transpose(2, 0, 1, 4, 3).reshape(NB * YT, K, BL)
    half = (lax.axis_index("lat") % 2 * 64).astype(I32).reshape(1)
    first, hi, lo, *sides, found, start, count = first_step(
        state, outflow, rows, owner, path_column, path_level, halo
    )
    sums = weigh(start, count, half, found, arrived)
    sensitivity = lax.all_to_all(sums, axes, 0, 0, tiled=True)[:, :CAP]
    final = last_step(first, outflow, exchange(*sides), (hi, lo))
    return final, sensitivity.reshape(OWN * CAP)


def solution(mesh):
    return jax.shard_map(
        body,
        mesh=mesh,
        in_specs=(
            P(None, None, "lat", "lon"),
            P(None, None, "lat", "lon"),
            P("lat", None, None, None),
            P(("lon", "lat"), None),
            P(("lon", "lat"), None),
            P(("lon", "lat"), None),
            P(None, ("lon", "lat")),
        ),
        out_specs=(P(None, None, "lat", "lon"), P(("lon", "lat"))),
        check_vma=False,
    )
```

```python
import jax
import jax.numpy as jnp
from jax import lax
from jax.experimental import pallas as pl
from jax.experimental.pallas import tpu as pltpu
from jax.sharding import PartitionSpec as P

T, L, NB, BL, Y, X = 3, 72, 3, 24, 32, 128
OWN, CAP, SND = 128, 64, 4096
YT = Y // 8
K = 8 * BL
ROWS = 40
GROUPS = SND // 128
ATTR = 11
F32, BF16, I32 = jnp.float32, jnp.bfloat16, jnp.int32
VMEM = 63 * 1024 * 1024


def params(*semantics):
    return pltpu.CompilerParams(vmem_limit_bytes=VMEM)


def shape(dims, dtype=F32):
    return jax.ShapeDtypeStruct(dims, dtype)


def iota(dims, dim):
    return lax.broadcasted_iota(I32, dims, dim)


def copies(pairs, sems):
    return [pltpu.make_async_copy(src, dst, sems.at[n]) for n, (src, dst) in enumerate(pairs)]


ANY = pl.BlockSpec(memory_space=pl.ANY)
IN_VMEM = pl.BlockSpec(memory_space=pltpu.VMEM)
IN_SMEM = pl.BlockSpec(memory_space=pltpu.SMEM)


def edge_columns(parts):
    lane = iota((parts[0].shape[0], X), 1)
    both = jnp.zeros(lane.shape, F32)
    for i, part in enumerate(parts):
        both = jnp.where(lane >> 1 == i, pltpu.roll(part, 2 * i + 1, 1), both)
    return both


PACKS = 4


def prepare_kernel(v_hbm, k_hbm, low_row, high_row, cols, packed_hbm, v, k, packed, v_sem, k_sem, p_sem):
    wide = OWN * CAP // PACKS
    deep = OWN // PACKS
    v_in = copies([(v_hbm.at[t], v.at[t]) for t in range(T)], v_sem)
    k_in = copies([(k_hbm.at[:, pl.ds(n * wide, wide)], k.at[n]) for n in range(PACKS)], k_sem)
    out = copies(
        [(packed.at[n], packed_hbm.at[pl.ds(n * deep, deep)]) for n in range(PACKS)], p_sem
    )
    for c in v_in + k_in:
        c.start()
    for t in range(T):
        v_in[t].wait()
        low_row[t] = v[t, pl.ds(0, L, stride=Y), :]
        high_row[t] = v[t, pl.ds(Y - 1, L, stride=Y), :]
        for b in range(NB):
            cols[b, t] = edge_columns([v[t, pl.ds((b * BL + i) * Y, Y), :] for i in range(BL)])
    first = iota((8, 128), 1) < 64
    for n in range(PACKS):
        k_in[n].wait()
        for pair in range(deep // 2):
            lanes = slice(pair * 128, (pair + 1) * 128)
            for r in range(5):
                low = k[n, r * 8 : r * 8 + 8, lanes]
                if r < 4:
                    high = pltpu.roll(k[n, (r + 5) * 8 : (r + 6) * 8, lanes], 64, 1)
                else:
                    high = jnp.zeros((8, 128), F32)
                packed[n, 2 * pair, r * 8 : r * 8 + 8, :] = jnp.where(first, low, high)
                packed[n, 2 * pair + 1, r * 8 : r * 8 + 8, :] = jnp.where(first, high, low)
        out[n].start()
    for c in out:
        c.wait()


def prepare(state, weights):
    return pl.pallas_call(
        prepare_kernel,
        in_specs=[ANY, ANY],
        out_specs=[IN_VMEM, IN_VMEM, IN_VMEM, ANY],
        out_shape=[
            shape((T, L, X)),
            shape((T, L, X)),
            shape((NB, T, Y, X)),
            shape((OWN, ROWS, 128)),
        ],
        scratch_shapes=[
            pltpu.VMEM((T, L * Y, X), F32),
            pltpu.VMEM((PACKS, L, OWN * CAP // PACKS), F32),
            pltpu.VMEM((PACKS, OWN // PACKS, ROWS, 128), F32),
            pltpu.SemaphoreType.DMA((T,)),
            pltpu.SemaphoreType.DMA((PACKS,)),
            pltpu.SemaphoreType.DMA((PACKS,)),
        ],
        compiler_params=params(),
        name="prepare",
    )(state.reshape(T, L * Y, X), weights)


def exchange(low_row, high_row, cols):
    lats, lons = lax.axis_size("lat"), lax.axis_size("lon")
    up = [(i, i + 1) for i in range(lats - 1)]
    down = [(b, a) for a, b in up]
    east = [(i, (i + 1) % lons) for i in range(lons)]
    west = [(b, a) for a, b in east]
    north = lax.ppermute(low_row, "lat", down)
    south = lax.ppermute(high_row, "lat", up)
    from_east = lax.ppermute(cols, "lon", west)
    from_west = lax.ppermute(cols, "lon", east)
    return north, south, from_east, from_west


def split(x):
    hi = x.astype(BF16)
    return hi, (x - hi.astype(F32)).astype(BF16)


def spread(r_ref, hi_ref, lo_ref):
    same = iota((K, K), 0) % 8 == iota((K, K), 1) % 8
    pick = jnp.where(iota((BL, K), 0) == iota((BL, K), 1) // 8, 1.0, 0.0).astype(BF16)
    for n in range(NB * YT):
        r = jnp.concatenate([r_ref[n, pl.ds(j, 8, stride=BL), :] for j in range(BL)], axis=0)
        for part, ref in zip(split(r), (hi_ref, lo_ref)):
            wide = jnp.dot(part, pick, preferred_element_type=F32)
            ref[n] = jnp.where(same, wide, 0.0).astype(BF16)


def transported(v, flows, north, south, sides):
    row, lane = iota((Y, X), 0), iota((Y, X), 1)
    e = pltpu.roll(jnp.where(lane == 0, sides, v), X - 1, 1)
    w = pltpu.roll(jnp.where(lane == X - 1, sides, v), 1, 1)
    n = jnp.where(row == Y - 1, north, pltpu.roll(v, Y - 1, 0))
    s = jnp.where(row == 0, south, pltpu.roll(v, 1, 0))
    return v + flows[0] * (e - v) + flows[1] * (w - v) + flows[2] * (n - v) + flows[3] * (s - v)


def mixed(hi, lo, x):
    x_hi, x_lo = split(x)
    dot = lambda a, b: jnp.dot(a, b, preferred_element_type=F32)
    return dot(hi, x_hi) + (dot(hi, x_lo) + dot(lo, x_hi))


def transport_block(adv, v, f, n_ref, s_ref, e_ref, w_ref):
    odd = (iota((Y, X), 1) & 1) == 1
    for t in range(T):
        sides = jnp.where(odd, e_ref[t], w_ref[t])
        for i in range(BL):
            a = transported(
                v[t, i],
                [f[k, i] for k in range(4)],
                n_ref[t, pl.ds(i, 1), :],
                s_ref[t, pl.ds(i, 1), :],
                pltpu.roll(sides, (X - 2 * i - 1) % X, 1),
            )
            for q in range(YT):
                adv[q, pl.ds(i * 8, 8), pl.ds(t * X, X)] = a[q * 8 : q * 8 + 8]


def tiles(out):
    return [[out[j * 8 : j * 8 + 8, t * X : (t + 1) * X] for j in range(BL)] for t in range(T)]


def last_kernel(v_ref, f_ref, n_ref, s_ref, e_ref, w_ref, hi_ref, lo_ref, out_ref, adv):
    transport_block(adv, v_ref, f_ref, n_ref, s_ref, e_ref, w_ref)
    for q in range(YT):
        parts = tiles(mixed(hi_ref[q], lo_ref[q], adv[q]))
        for t in range(T):
            for j in range(BL):
                out_ref[t, j, pl.ds(q * 8, 8), :] = parts[t][j]


def last_step(state, outflow, halo, matrices):
    return pl.pallas_call(
        last_kernel,
        grid=(NB,),
        in_specs=[
            pl.BlockSpec((T, BL, Y, X), lambda b: (0, b, 0, 0)),
            pl.BlockSpec((4, BL, Y, X), lambda b: (0, b, 0, 0)),
            pl.BlockSpec((T, BL, X), lambda b: (0, b, 0)),
            pl.BlockSpec((T, BL, X), lambda b: (0, b, 0)),
            pl.BlockSpec((None, T, Y, X), lambda b: (b, 0, 0, 0)),
            pl.BlockSpec((None, T, Y, X), lambda b: (b, 0, 0, 0)),
            pl.BlockSpec((YT, K, K), lambda b: (b, 0, 0)),
            pl.BlockSpec((YT, K, K), lambda b: (b, 0, 0)),
        ],
        out_specs=pl.BlockSpec((T, BL, Y, X), lambda b: (0, b, 0, 0)),
        out_shape=shape((T, L, Y, X)),
        scratch_shapes=[pltpu.VMEM((YT, K, T * X), F32)],
        compiler_params=params(),
        name="last_step",
    )(state, outflow, *halo, *matrices)


def order(own_ref, col_ref, lev_ref, pc_ref, pv_ref, start_ref, count_ref, place):
    width = 256
    chunks = SND // width
    owner = iota((OWN, width), 0)
    named = lambda c: owner == own_ref[:, pl.ds(c * width, width)]
    bit = lambda m: jnp.where(m, 1.0, 0.0).astype(BF16)
    upto = bit(iota((width, width), 0) <= iota((width, width), 1))
    ones = jnp.ones((width, width), BF16)
    ones_rows = jnp.ones((16, width), BF16)
    total = jnp.zeros((OWN, width), F32)
    total_row = jnp.zeros((16, OWN), F32)
    over_lanes = (((1,), (1,)), ((), ()))
    for c in range(chunks):
        hot = bit(named(c))
        total = total + jnp.dot(hot, ones, preferred_element_type=F32)
        total_row = total_row + lax.dot_general(
            ones_rows, hot, over_lanes, preferred_element_type=F32
        )
    below = bit(iota((OWN, OWN), 1) < iota((OWN, OWN), 0))
    before = bit(iota((OWN, OWN), 0) < iota((OWN, OWN), 1))
    base = jnp.dot(below, total.astype(BF16), preferred_element_type=F32)
    start_row = jnp.dot(total_row.astype(BF16), before, preferred_element_type=F32)
    start_ref[...] = start_row[0:1].astype(I32)
    count_ref[...] = total_row[0:1].astype(I32)
    for c in range(chunks):
        m = named(c)
        hot = bit(m)
        upto_here = jnp.dot(hot, upto, preferred_element_type=F32) + base
        spot = jnp.sum(jnp.where(m, upto_here, 0.0), axis=0, keepdims=True) - 1.0
        place[:, pl.ds(c * width, width)] = spot.astype(I32)
        base = base + jnp.dot(hot, ones, preferred_element_type=F32)
    width = 512
    sorted_ = jnp.zeros((ATTR * GROUPS, 128), F32)
    for c in range(SND // width):
        here = pl.ds(c * width, width)
        spot = place[:, here]
        group = iota((GROUPS, width), 0) == spot // 128
        lane = bit(iota((128, width), 0) == spot % 128)
        rows = []
        for a in range(4):
            rows.append(col_ref[a : a + 1, here] // 128)
        for a in range(4):
            rows.append(col_ref[a : a + 1, here] % 128)
        for a in range(3):
            rows.append(lev_ref[a : a + 1, here])
        spread_rows = jnp.concatenate(
            [jnp.where(group, r.astype(F32), 0.0) for r in rows], axis=0
        ).astype(BF16)
        sorted_ = sorted_ + lax.dot_general(
            spread_rows, lane, over_lanes, preferred_element_type=F32
        )
    for a in range(4):
        y = sorted_[a * GROUPS : (a + 1) * GROUPS]
        x = sorted_[(a + 4) * GROUPS : (a + 5) * GROUPS]
        pc_ref[a] = (y * 128.0 + x).astype(I32)
        pc_ref[a + 4] = pltpu.roll(pc_ref[a], 64, 1)
    for a in range(3):
        pv_ref[a] = sorted_[(a + 8) * GROUPS : (a + 9) * GROUPS].astype(I32)
        pv_ref[a + 3] = pltpu.roll(pv_ref[a], 64, 1)


def sample_all(table, pc_ref, pv_ref, found):
    def sample(g, carry):
        for k in range(L // 8):
            swap = 0 if k < 5 else 1
            cols = [pc_ref[a + 4 * swap, pl.ds(g, 1), :] for a in range(4)]
            levs = [pv_ref[a + 3 * swap, pl.ds(g, 1), :] for a in range(3)]
            level = iota((8, 128), 0) + k * 8
            passed = [jnp.where(v <= level, 1, 0) for v in levs]
            element = passed[0] + passed[1] + passed[2]
            at = jnp.where(
                element < 2,
                jnp.where(element < 1, cols[0], cols[1]),
                jnp.where(element < 3, cols[2], cols[3]),
            )
            x, y = at & 127, at >> 7
            acc = jnp.zeros((8, 128), F32)
            for row in range(Y):
                got = jnp.take_along_axis(
                    table[row, k * 8 : k * 8 + 8, :], x, axis=1, mode="promise_in_bounds"
                )
                acc = jnp.where(y == row, got, acc)
            found[g, k * 8 : k * 8 + 8, :] = acc
        return carry

    lax.fori_loop(0, GROUPS, sample, 0)
    found[GROUPS] = jnp.zeros((L, 128), F32)


def first_kernel(
    v_hbm, f_hbm, r_ref, own_ref, col_ref, lev_ref, n_ref, s_ref, e_ref, w_ref,
    out_hbm, hi_hbm, lo_hbm, low_row, high_row, cols, found, start_ref, count_ref,
    v, f, out, hi, lo, table, adv, summed, pc, pv, place, v_sem, f_sem, o_sem, m_sem,
):
    levels = [pl.ds(b * BL, BL) for b in range(NB)]
    v_in = copies([(v_hbm.at[:, d], v.at[b]) for b, d in enumerate(levels)], v_sem)
    f_in = copies([(f_hbm.at[:, d], f.at[b]) for b, d in enumerate(levels)], f_sem)
    outs = copies([(out.at[b], out_hbm.at[:, d]) for b, d in enumerate(levels)], o_sem)
    made = copies([(hi, hi_hbm), (lo, lo_hbm)], m_sem)
    for b in range(NB):
        v_in[b].start()
        f_in[b].start()
    spread(r_ref, hi, lo)
    for c in made:
        c.start()
    order(own_ref, col_ref, lev_ref, pc, pv, start_ref, count_ref, place)
    for b in range(NB):
        v_in[b].wait()
        f_in[b].wait()
        here = levels[b]
        transport_block(
            adv, v.at[b], f.at[b], n_ref.at[:, here], s_ref.at[:, here], e_ref.at[b], w_ref.at[b]
        )
        for q in range(YT):
            parts = tiles(mixed(hi[b * YT + q], lo[b * YT + q], adv[q]))
            rows = pl.ds(q * 8, 8)
            for t in range(T):
                for j in range(BL):
                    out[b, t, j, rows, :] = parts[t][j]
            for j in range(BL):
                summed[pl.ds(j * Y + q * 8, 8), :] = parts[0][j] + parts[1][j] + parts[2][j]
        for y in range(Y):
            table[y, here, :] = summed[pl.ds(y, BL, stride=Y), :]
        for t in range(T):
            low_row[t, here, :] = out[b, t, :, 0, :]
            high_row[t, here, :] = out[b, t, :, Y - 1, :]
        outs[b].start()
    lane = iota((Y, X), 1)

    def columns(i, both):
        here = lane >> 1 == i
        return tuple(
            jnp.where(here, pltpu.roll(out[n // T, n % T, i], 2 * i + 1, 1), both[n])
            for n in range(NB * T)
        )

    both = lax.fori_loop(0, BL, columns, (jnp.zeros((Y, X), F32),) * (NB * T))
    for n in range(NB * T):
        cols[n // T, n % T] = both[n]
    sample_all(table, pc, pv, found)
    for c in outs + made:
        c.wait()


def first_step(state, outflow, rows, owner, path_column, path_level, halo):
    vmem = lambda dims, dtype=F32: pltpu.VMEM(dims, dtype)
    return pl.pallas_call(
        first_kernel,
        in_specs=[ANY, ANY] + [IN_VMEM] * 8,
        out_specs=[ANY, ANY, ANY] + [IN_VMEM] * 6,
        out_shape=[
            shape((T, L, Y, X)),
            shape((NB * YT, K, K), BF16),
            shape((NB * YT, K, K), BF16),
            shape((T, L, X)),
            shape((T, L, X)),
            shape((NB, T, Y, X)),
            shape((GROUPS + 1, L, 128)),
            shape((1, OWN), I32),
            shape((1, OWN), I32),
        ],
        scratch_shapes=[
            vmem((NB, T, BL, Y, X)),
            vmem((NB, 4, BL, Y, X)),
            vmem((NB, T, BL, Y, X)),
            vmem((NB * YT, K, K), BF16),
            vmem((NB * YT, K, K), BF16),
            vmem((Y, L, X)),
            vmem((YT, K, T * X)),
            vmem((BL * Y, X)),
            vmem((8, GROUPS, 128), I32),
            vmem((6, GROUPS, 128), I32),
            vmem((1, SND), I32),
            pltpu.SemaphoreType.DMA((NB,)),
            pltpu.SemaphoreType.DMA((NB,)),
            pltpu.SemaphoreType.DMA((NB,)),
            pltpu.SemaphoreType.DMA((2,)),
        ],
        compiler_params=params(),
        name="first_step",
    )(state, outflow, rows, owner.reshape(1, SND), path_column.T, path_level.T, *halo)


def weigh_kernel(
    start_ref, count_ref, half_ref, found_hbm, k_hbm, out_ref, found, k, kept, found_sem, k_sem
):
    deep = OWN // PACKS
    k_in = copies([(k_hbm.at[pl.ds(c * deep, deep)], k.at[c]) for c in range(PACKS)], k_sem)
    (found_in,) = copies([(found_hbm, found)], found_sem)
    found_in.start()
    for c in k_in:
        c.start()
    found_in.wait()
    lane = iota((8, 128), 1)
    many = 16
    for c in range(PACKS):
        k_in[c].wait()

        def some(step, carry):
            sums = []
            for n in range(many):
                o = c * deep + step * many + n
                start, count = start_ref[0, o], count_ref[0, o]
                group, offset = jnp.minimum(start >> 7, GROUPS - 1), start & 127
                near = lane >= offset
                near_high = (lane ^ 64) >= offset
                low = ((lane - offset) & 127) < 64
                acc = jnp.zeros((8, 128), F32)
                for r in range(5):
                    rows = slice(r * 8, r * 8 + 8)
                    z = jnp.where(near, found[group, rows, :], found[group + 1, rows, :])
                    if r < 4:
                        high = slice((r + 5) * 8, (r + 6) * 8)
                        z_high = jnp.where(
                            near_high, found[group, high, :], found[group + 1, high, :]
                        )
                        z = jnp.where(low, z, z_high)
                    turned = pltpu.roll(z, (half_ref[0] + 128 - offset) & 127, 1)
                    acc = acc + turned * k[c, step * many + n, rows, :]
                sums.append(jnp.where((lane & 63) < count, acc, 0.0))
            for n in range(many):
                kept[pl.ds((c * deep + step * many + n) * 8, 8), :] = sums[n]
            return carry

        lax.fori_loop(0, deep // many, some, 0)
    total = kept[pl.ds(0, OWN, stride=8), :]
    for r in range(1, 8):
        total = total + kept[pl.ds(r, OWN, stride=8), :]
    out_ref[...] = total + pltpu.roll(total, 64, 1)


def weigh(start, count, half, found, arrived):
    return pl.pallas_call(
        weigh_kernel,
        in_specs=[IN_SMEM, IN_SMEM, IN_SMEM, ANY, ANY],
        out_specs=IN_VMEM,
        out_shape=shape((OWN, 128)),
        scratch_shapes=[
            pltpu.VMEM((GROUPS + 1, L, 128), F32),
            pltpu.VMEM((PACKS, OWN // PACKS, ROWS, 128), F32),
            pltpu.VMEM((OWN * 8, 128), F32),
            pltpu.SemaphoreType.DMA((1,)),
            pltpu.SemaphoreType.DMA((PACKS,)),
        ],
        compiler_params=params(),
        name="weigh",
    )(start, count, half, found, arrived)


def body(state, outflow, mix_blocks, owner, path_column, path_level, weights):
    axes = ("lon", "lat")
    *sides, packed = prepare(state, weights)
    packed, halo = lax.optimization_barrier((packed, exchange(*sides)))
    arrived = lax.all_to_all(packed, axes, 0, 0, tiled=True)
    rows = mix_blocks.reshape(YT, 8, NB, BL, BL).transpose(2, 0, 1, 4, 3).reshape(NB * YT, K, BL)
    half = (lax.axis_index("lat") % 2 * 64).astype(I32).reshape(1)
    first, hi, lo, *sides, found, start, count = first_step(
        state, outflow, rows, owner, path_column, path_level, halo
    )
    sums = weigh(start, count, half, found, arrived)
    sensitivity = lax.all_to_all(sums, axes, 0, 0, tiled=True)[:, :CAP]
    final = last_step(first, outflow, exchange(*sides), (hi, lo))
    return final, sensitivity.reshape(OWN * CAP)


def solution(mesh):
    return jax.shard_map(
        body,
        mesh=mesh,
        in_specs=(
            P(None, None, "lat", "lon"),
            P(None, None, "lat", "lon"),
            P("lat", None, None, None),
            P(("lon", "lat"), None),
            P(("lon", "lat"), None),
            P(("lon", "lat"), None),
            P(None, ("lon", "lat")),
        ),
        out_specs=(P(None, None, "lat", "lon"), P(("lon", "lat"))),
        check_vma=False,
    )
```
